32 devices in a mesh: rows: 8 (over z, x), tensor: 4 (over y, core).
Axes of the slice: x: 2, y: 2, z: 4, core: 2. Of those that a mesh axis runs over, the one named last changes fastest.
Arguments:
- context: bfloat16 [2, 1280, 4096], P(None, 'rows', 'tensor'), may hold values from -6 to 6
- o_weight: bfloat16 [4096, 8192], P('tensor'), may hold values from -0.125 to 0.125
- residual: bfloat16 [2, 1280, 8192], P(None, 'rows', 'tensor'), may hold values from -6 to 6
- counts: int32 [2, 256], P(None, 'rows'), may hold values from 0 to 5
- slots: int32 [2, 1280], P(None, 'rows'), may hold values from 0 to 1279, as said below
- fc_weight: bfloat16 [2048, 8192], P('rows', 'tensor'), may hold values from -0.0625 to 0.0625
- gain: float32 [2048], replicated, may hold values from 0.1 to 1.9
- goal: bfloat16 [2, 1280, 2048], P(None, 'rows'), may hold values from -6 to 6
Outputs:
- verified: float32 [2, 1280, 8192], P(None, 'rows', 'tensor')
- draft_out: float32 [2, 1280, 2048], P(None, 'rows', 'tensor')
- fc_grad: float32 [2048, 8192], P('rows', 'tensor')
The draws below stay inside these ranges and needn't reach their ends.
Inputs may be any that keep to these rules, and one draw needn't show every extreme that they name: In each step the slots of all rows are a permutation of 0 to 1279. Slot i belongs to trainer device i // 160; the rows of device p take, on every trainer device, exactly the 20 slots from p * 20 to (p + 1) * 20 - 1 of that device's block.
All inputs are finite; a program needn't handle non-finite values.
Results may differ from the reference program's by a relative error of at most 0.014.
Values may be sent and summed in bfloat16 or wider, within the bound.
A program may use at most 128 MiB of HBM per device.

```python
import math
import jax
import jax.numpy as jnp
from jax import lax

D = 8192
DRAFT = 2048
K = 5
STEPS = 2
ROWS_DEV = 160
REQS = 256
ROWS = 1280
QWIDTH = 4096
N_TENSOR = 4


def one_order(subkey):
    return jax.random.permutation(subkey, ROWS_DEV)


def draw_slots(key, part):
    device_count = ROWS // ROWS_DEV
    per_peer = ROWS_DEV // device_count
    keys = jax.random.split(key, STEPS * device_count)
    orders = jax.vmap(one_order)(keys).astype(jnp.int32)
    orders = orders.reshape(STEPS, device_count, ROWS_DEV)
    source = jnp.arange(device_count, dtype=jnp.int32)[None, :, None]
    placed = orders // per_peer * ROWS_DEV + source * per_peer + orders % per_peer
    return placed.reshape(STEPS, ROWS).astype(jnp.int32)


def touch_ends(array, stream_key, least, high):
    shape = array.shape
    place = [jax.random.randint(jax.random.fold_in(stream_key, axis), (), 0, shape[axis]) for axis in range(len(shape))]
    array = array.at[tuple(place)].set(least)
    longest = shape.index(max(shape))
    place[longest] = (place[longest] + 1) % shape[longest]
    return array.at[tuple(place)].set(high)


def with_spikes(entries, key, source, target, shards_of, factor):
    def block_of(axis_at):
        return (jnp.arange(entries.shape[axis_at]) // (entries.shape[axis_at] // shards_of)).reshape((-1,) + (1,) * (entries.ndim - 1 - axis_at))

    near = jax.random.permutation(key, shards_of)[block_of(target)]
    other_side = (block_of(target) + shards_of // 2) % shards_of
    return jnp.where((block_of(source) == near) | (block_of(source) == other_side), factor * entries, entries)


def steps_of(own_key, dims, pieces, smallest, top_value):
    def one(position, parts):
        draws = jax.random.uniform(jax.random.fold_in(jax.random.fold_in(own_key, 6), position), (parts,), jnp.float32, smallest / len(pieces), top_value / len(pieces))
        return jnp.repeat(jnp.exp(draws), dims[position] // parts).reshape((-1,) + (1,) * (len(dims) - position - 1))

    level = one(*pieces[0])
    for cut in pieces[1:]:
        level = level * one(*cut)
    return level


def noise(rng, dims, deviation, reach, cuts=(), held_as=jnp.bfloat16):
    level = steps_of(rng, dims, cuts, -0.22, 0.18) if cuts else 1.0
    array = jax.random.normal(rng, dims, jnp.float32) * deviation * level
    return jnp.minimum(jnp.maximum(array, -reach), reach).astype(held_as)


def bell_draw_with(rng, extent, scale, limit, pieces, heavy, kind=jnp.bfloat16):
    values = scale * jax.random.normal(rng, extent, jnp.float32)
    if pieces:
        values = values * steps_of(rng, extent, pieces, -0.22, 0.18)
    return jnp.clip(with_spikes(values, jax.random.fold_in(rng, 3), *heavy), -limit, limit).astype(kind)


def setup_inputs(seed: int = 0) -> dict:
    key_list = jax.random.split(jax.random.key(seed), 9)
    return {
        "context": noise(key_list[0], (STEPS, ROWS, QWIDTH), 1.0, 6.0, ((1, 8), (2, 4))),
        "o_weight": bell_draw_with(key_list[1], (QWIDTH, D), QWIDTH ** -0.5, 0.125, ((0, 4),), (0, 1, 4, 2.0)),
        "residual": noise(key_list[2], (STEPS, ROWS, D), 1.0, 6.0, ((1, 8), (2, 4))),
        "counts": touch_ends(jax.random.randint(key_list[3], (STEPS, REQS), 0, K + 1), jax.random.fold_in(key_list[3], 1), 0, K).astype(jnp.int32),
        "slots": draw_slots(jax.random.fold_in(key_list[8], 71), 0),
        "fc_weight": noise(key_list[5], (DRAFT, D), D ** -0.5, 0.0625, ((0, 8), (1, 4))),
        "gain": jnp.clip(1.0 + 0.18 * jax.random.normal(key_list[6], (DRAFT,), jnp.float32), 0.1, 1.9),
        "goal": noise(key_list[7], (STEPS, ROWS, DRAFT), 1.0, 6.0, ((1, 8),)),
    }


epsilon = 1e-06

def draft_norm(summed, gain, goal, weight):
    mean_square = lax.optimization_barrier(jnp.mean(summed * summed, axis=-1, keepdims=True))
    inverse = lax.rsqrt(mean_square + epsilon)
    normed = summed * inverse * gain
    error = normed - goal.astype(jnp.float32)
    pulled = gain * (weight * error)
    spread = lax.optimization_barrier(jnp.mean(summed * pulled, axis=-1, keepdims=True))
    back = inverse * (pulled - summed * (inverse * inverse) * spread)
    return (normed, back.astype(jnp.bfloat16))

def reference(context, o_weight, residual, counts, slots, fc_weight, gain, goal):
    block = QWIDTH // N_TENSOR
    weight = 1.0 / math.sqrt(STEPS * ROWS)
    offsets = jnp.arange(ROWS, dtype=jnp.int32) % K
    verified = []
    drafted = []
    grad = jnp.zeros((DRAFT, D), jnp.float32)
    for step in range(STEPS):
        projected = jnp.zeros((ROWS, D), jnp.float32)
        for shard in range(N_TENSOR):
            head_terms = jnp.dot(context[step][:, shard * block:(shard + 1) * block], o_weight[shard * block:(shard + 1) * block], preferred_element_type=jnp.float32)
            rounded = lax.optimization_barrier(head_terms.astype(jnp.bfloat16))
            projected = projected + rounded.astype(jnp.float32)
        full_state = residual[step].astype(jnp.float32) + projected
        verified.append(full_state)
        hidden = full_state.astype(jnp.bfloat16)
        accepted = offsets < jnp.repeat(counts[step], K)
        masked = jnp.where(accepted[:, None], hidden, jnp.zeros_like(hidden))
        trained = jnp.zeros_like(masked).at[slots[step]].set(masked)
        summed = jnp.dot(trained, fc_weight.T, preferred_element_type=jnp.float32)
        normed, back = draft_norm(summed, gain, goal[step], weight)
        drafted.append(normed)
        grad = grad + jnp.dot(back.T, trained, preferred_element_type=jnp.float32)
    return (jnp.stack(verified), jnp.stack(drafted), grad)
```

```python
import math

import jax
import jax.numpy as jnp
from jax import lax
from jax.sharding import PartitionSpec as P

K = 5
epsilon = 1e-06


def local(context, o_weight, residual, counts, slots, fc_weight, gain, goal):
    steps = context.shape[0]
    row_count = lax.axis_size("rows")
    inner = lax.axis_size("tensor")
    outer = row_count // inner
    rows_dev = context.shape[1]
    width = residual.shape[2]
    block = fc_weight.shape[0]
    draft = goal.shape[2]
    per_peer = rows_dev // row_count
    source = lax.axis_index("rows")
    column = lax.axis_index("tensor")
    hi = source // inner
    lo = source % inner
    weight = 1.0 / math.sqrt(steps * rows_dev * row_count)
    groups = [[h * inner + l for l in range(inner)] for h in range(outer)]
    shifts = [
        [(r, (r + k * inner) % row_count) for r in range(row_count)] for k in range(outer)
    ]

    weights = [fc_weight] + [lax.ppermute(fc_weight, "rows", shifts[k]) for k in range(1, outer)]
    weights = jnp.concatenate(weights, 0)
    relative = (jnp.arange(outer)[:, None] - jnp.arange(outer)[None, :]) % outer
    goal_part = lax.dynamic_index_in_dim(
        goal.reshape(steps, outer, inner, per_peer, outer, inner, block), column, 2, False
    )
    goal_out = jnp.stack(
        [
            jnp.stack([goal_part[:, h, :, (h - k) % outer] for k in range(outer)], 2)
            for h in range(outer)
        ],
        0,
    )
    goal_out = jnp.transpose(goal_out, (0, 4, 1, 2, 3, 5)).reshape(
        row_count, steps, per_peer, outer * block
    )
    goal_in = lax.all_to_all(goal_out, "rows", split_axis=0, concat_axis=0, tiled=True)
    goal_in = jnp.transpose(goal_in, (1, 0, 2, 3)).reshape(steps * rows_dev, outer * block)
    gain_own = gain.reshape(outer, inner, block)[relative[hi], lo].reshape(1, outer * block)

    offsets = jnp.arange(rows_dev, dtype=jnp.int32) % K
    verified = []
    hidden_rows = []
    for step in range(steps):
        head_terms = jnp.dot(context[step], o_weight, preferred_element_type=jnp.float32)
        projected = lax.psum_scatter(
            head_terms.astype(jnp.bfloat16), "tensor", scatter_dimension=1, tiled=True
        ).astype(jnp.float32)
        full_state = residual[step].astype(jnp.float32) + projected
        verified.append(full_state)
        hidden = full_state.astype(jnp.bfloat16)
        accepted = offsets < jnp.repeat(counts[step], K)
        slot_ids = slots[step]
        position = slot_ids // rows_dev * per_peer + slot_ids % rows_dev - source * per_peer
        place = (position[None, :] == jnp.arange(rows_dev)[:, None]) & accepted[None, :]
        moved = jnp.dot(
            place.astype(jnp.bfloat16), hidden, preferred_element_type=jnp.float32
        ).astype(jnp.bfloat16)
        hidden_rows.append(
            lax.all_gather(moved, "rows", axis=0, tiled=False, axis_index_groups=groups)
        )
    trained = jnp.stack(hidden_rows, 1).reshape(inner * steps * rows_dev, width)
    terms = lax.dot_general(
        trained, weights, (((1,), (1,)), ((), ())), preferred_element_type=jnp.float32
    ).astype(jnp.bfloat16)
    summed = lax.psum_scatter(terms, "tensor", scatter_dimension=0, tiled=True).astype(jnp.float32)
    goal_rows = goal_in.astype(jnp.float32)
    scaled = summed * gain_own
    stats = jnp.stack(
        [
            jnp.sum(summed * summed, -1),
            jnp.sum(scaled * scaled, -1),
            jnp.sum(scaled * goal_rows, -1),
        ]
    )
    stats = jnp.sum(
        lax.all_gather(stats, "rows", axis=0, tiled=False, axis_index_groups=groups), 0
    )
    inverse = lax.rsqrt(stats[0] / draft + epsilon)
    spread = weight * (inverse * stats[1] - stats[2]) / draft
    inverse = inverse[:, None]
    spread = spread[:, None]
    normed = scaled * inverse
    pulled = gain_own * (weight * (normed - goal_rows))
    back_share = (inverse * (pulled - summed * (inverse * inverse) * spread)).astype(jnp.bfloat16)
    back = lax.all_gather(back_share, "tensor", axis=0, tiled=True)
    grad_terms = []
    for k in range(outer):
        grad_terms.append(
            lax.dot_general(
                back[:, k * block : (k + 1) * block],
                trained,
                (((0,), (0,)), ((), ())),
                preferred_element_type=jnp.float32,
            )
        )
    grad = grad_terms[0]
    for k in range(1, outer):
        back_shift = [(b, a) for a, b in shifts[k]]
        grad = grad + lax.ppermute(
            grad_terms[k].astype(jnp.bfloat16), "rows", back_shift
        ).astype(jnp.float32)

    out = normed.astype(jnp.bfloat16).reshape(steps, row_count, per_peer, outer * block)
    out = lax.all_to_all(
        jnp.transpose(out, (1, 0, 2, 3)), "rows", split_axis=0, concat_axis=0, tiled=True
    ).reshape(outer, inner, steps, per_peer, outer, block)
    out = jnp.stack(
        [
            jnp.stack([out[h, :, :, :, (h - a) % outer] for a in range(outer)], 0)
            for h in range(outer)
        ],
        0,
    )
    out = jnp.transpose(out, (1, 2, 5, 3, 0, 4))
    out = jnp.transpose(
        out.reshape(inner, draft // inner, steps, outer, per_peer), (0, 2, 3, 4, 1)
    )
    out = lax.all_to_all(out, "tensor", split_axis=0, concat_axis=0, tiled=True)
    draft_out = (
        jnp.transpose(out, (1, 2, 0, 3, 4))
        .reshape(steps, rows_dev, draft // inner)
        .astype(jnp.float32)
    )
    return (jnp.stack(verified), draft_out, grad)


def solution(mesh):
    placed = (
        P(None, "rows", "tensor"),
        P("tensor", None),
        P(None, "rows", "tensor"),
        P(None, "rows"),
        P(None, "rows"),
        P("rows", "tensor"),
        P(),
        P(None, "rows", None),
    )
    return jax.shard_map(
        local,
        mesh=mesh,
        in_specs=placed,
        out_specs=(P(None, "rows", "tensor"), P(None, "rows", "tensor"), P("rows", "tensor")),
        check_vma=False,
    )
```

```python
import functools
import math

import jax
import jax.numpy as jnp
from jax import lax
from jax.experimental import pallas as pl
from jax.experimental.pallas import tpu as pltpu
from jax.sharding import PartitionSpec as P

K = 5
epsilon = 1e-06


CHUNKS = 4
LANES = 128
STAT_ROWS = 8
MESH = pl.DeviceIdType.MESH


def kernel(
    sizes, weight, draft,
    ctx, ow_hbm, res, place, fcw, goal, gain,
    verified, trained, normed_out, back_out,
    ow, sendp, recvp, hbuf, wbuf, sends, recvs, stat_send, stat_recv, backbuf,
    ow_sem, p_send, p_recv, h_send, h_recv, w_send, w_recv,
    s_send, s_recv, t_send, t_recv, b_send, b_recv, out_sem,
):
    row_count, inner, outer, steps = sizes
    rows, width = res.shape
    half = rows // steps
    chunk = width // CHUNKS
    block = fcw.shape[0]
    me = lax.axis_index("rows")
    column = lax.axis_index("tensor")
    hi = me // inner
    lo = me % inner

    def tensor_peer(j):
        return (me, (column + j) % inner)

    def lo_peer(j):
        return (hi * inner + (lo + j) % inner, column)

    def hi_peer(k):
        return ((me + k * inner) % row_count, column)

    order = [inner // 2] + [j for j in range(1, inner) if j != inner // 2]

    def ow_copy(c, j):
        owner = (column + j) % inner
        start = pl.multiple_of(owner * width + c * chunk, chunk)
        return pltpu.make_async_copy(
            ow_hbm.at[:, pl.ds(start, chunk)], ow.at[c, j], ow_sem.at[c, j]
        )

    for c in range(CHUNKS):
        for j in order + [0]:
            ow_copy(c, j).start()

    barrier = pltpu.get_barrier_semaphore()
    for j in range(1, inner):
        pl.semaphore_signal(barrier, inc=1, device_id=tensor_peer(j), device_id_type=MESH)
        pl.semaphore_signal(barrier, inc=1, device_id=lo_peer(j), device_id_type=MESH)
    for k in range(1, outer):
        pl.semaphore_signal(barrier, inc=1, device_id=hi_peer(k), device_id_type=MESH)
    pl.semaphore_wait(barrier, 2 * (inner - 1) + outer - 1)

    def remote(src, dst, send_sem, recv_sem, device):
        return pltpu.make_async_remote_copy(
            src_ref=src, dst_ref=dst, send_sem=send_sem, recv_sem=recv_sem,
            device_id=device, device_id_type=MESH,
        )

    def w_copy(k):
        return remote(fcw, wbuf.at[k - 1], w_send.at[k - 1], w_recv.at[k - 1], hi_peer(k))

    def p_copy(c, j):
        return remote(
            sendp.at[c, j - 1], recvp.at[c, j - 1], p_send.at[c, j - 1], p_recv.at[c, j - 1],
            tensor_peer(j),
        )

    def h_copy(c, j, owner):
        part = hbuf.at[owner, :, pl.ds(c * chunk, chunk)]
        return remote(part, part, h_send.at[c, j - 1], h_recv.at[c, j - 1], lo_peer(j))

    def s_copy(j):
        return remote(
            sends.at[j - 1], recvs.at[j - 1], s_send.at[j - 1], s_recv.at[j - 1], tensor_peer(j)
        )

    def t_copy(j):
        return remote(
            stat_send, stat_recv.at[j - 1], t_send.at[j - 1], t_recv.at[j - 1], lo_peer(j)
        )

    def b_copy(j, owner):
        return remote(
            backbuf.at[owner], backbuf.at[owner], b_send.at[j - 1], b_recv.at[j - 1],
            tensor_peer(j),
        )

    for k in range(1, outer):
        w_copy(k).start()

    def product(c, j):
        ow_copy(c, j).wait()
        return jnp.dot(ctx[...], ow[c, j], preferred_element_type=jnp.float32).astype(
            jnp.bfloat16
        )

    def finish(c):
        cols = pl.ds(c * chunk, chunk)
        total = product(c, 0).astype(jnp.float32)
        for j in range(1, inner):
            p_copy(c, j).wait_recv()
            total = total + recvp[c, j - 1].astype(jnp.float32)
        total = total + res[:, cols].astype(jnp.float32)
        verified[:, cols] = total
        hidden = total.astype(jnp.bfloat16)
        for step in range(steps):
            hbuf[lo, pl.ds(step * half, half), cols] = jnp.dot(
                place[step], hidden[step * half : (step + 1) * half],
                preferred_element_type=jnp.float32,
            ).astype(jnp.bfloat16)
        for j in range(1, inner):
            h_copy(c, j, lo).start()

    for c in range(CHUNKS):
        for j in order:
            sendp[c, j - 1] = product(c, j)
            p_copy(c, j).start()
        if c >= 1:
            finish(c - 1)
    finish(CHUNKS - 1)

    for j in range(1, inner):
        for c in range(CHUNKS):
            h_copy(c, j, (lo - j + inner) % inner).wait_recv()
    for k in range(1, outer):
        w_copy(k).wait_recv()

    out_copy = pltpu.make_async_copy(hbuf, trained, out_sem)
    out_copy.start()

    def sums(j):
        mine = hbuf[(column + j) % inner]
        parts = [
            lax.dot_general(
                mine, w, (((1,), (1,)), ((), ())), preferred_element_type=jnp.float32
            )
            for w in [fcw[...]] + [wbuf[k - 1] for k in range(1, outer)]
        ]
        return jnp.concatenate(parts, 1).astype(jnp.bfloat16)

    for j in order:
        sends[j - 1] = sums(j)
        s_copy(j).start()
    summed = sums(0).astype(jnp.float32)
    for j in range(1, inner):
        s_copy(j).wait_recv()
        summed = summed + recvs[j - 1].astype(jnp.float32)
    goal_rows = goal[...].astype(jnp.float32)
    gains = gain[...]
    scaled = summed * gains
    lane = lax.broadcasted_iota(jnp.int32, (rows, LANES), 1)
    stats = jnp.where(
        lane == 0,
        jnp.sum(summed * summed, -1, keepdims=True),
        jnp.where(
            lane == 1,
            jnp.sum(scaled * scaled, -1, keepdims=True),
            jnp.sum(scaled * goal_rows, -1, keepdims=True),
        ),
    )
    padded = stat_send.shape[1]
    if padded > rows:
        stats = jnp.concatenate([stats, jnp.zeros((padded - rows, LANES), jnp.float32)], 0)
    stat_send[...] = jnp.transpose(stats)[:STAT_ROWS]
    for j in range(1, inner):
        t_copy(j).start()
    total = stat_send[...]
    for j in range(1, inner):
        t_copy(j).wait_recv()
        total = total + stat_recv[j - 1]
    total = jnp.transpose(
        jnp.concatenate([total, jnp.zeros((LANES - STAT_ROWS, padded), jnp.float32)], 0)
    )[:rows]
    inverse = lax.rsqrt(total[:, 0:1] / draft + epsilon)
    spread = weight * (inverse * total[:, 1:2] - total[:, 2:3]) / draft
    normed = scaled * inverse
    pulled = gains * (weight * (normed - goal_rows))
    backbuf[column] = (inverse * (pulled - summed * (inverse * inverse) * spread)).astype(
        jnp.bfloat16
    )
    for j in range(1, inner):
        b_copy(j, column).start()
    normed_out[...] = normed.astype(jnp.bfloat16)
    for j in range(1, inner):
        b_copy(j, (column - j + inner) % inner).wait_recv()
    back_out[...] = backbuf[...]

    for k in range(1, outer):
        w_copy(k).wait_send()
    for j in range(1, inner):
        for c in range(CHUNKS):
            p_copy(c, j).wait_send()
            h_copy(c, j, lo).wait_send()
        s_copy(j).wait_send()
        t_copy(j).wait_send()
        b_copy(j, column).wait_send()
    out_copy.wait()


def local(context, o_weight, residual, counts, slots, fc_weight, gain, goal):
    steps = context.shape[0]
    row_count = lax.axis_size("rows")
    inner = lax.axis_size("tensor")
    outer = row_count // inner
    rows_dev = context.shape[1]
    width = residual.shape[2]
    block = fc_weight.shape[0]
    draft = goal.shape[2]
    per_peer = rows_dev // row_count
    source = lax.axis_index("rows")
    column = lax.axis_index("tensor")
    hi = source // inner
    lo = source % inner
    weight = 1.0 / math.sqrt(steps * rows_dev * row_count)
    shifts = [
        [(r, (r + k * inner) % row_count) for r in range(row_count)] for k in range(outer)
    ]

    relative = (jnp.arange(outer)[:, None] - jnp.arange(outer)[None, :]) % outer
    goal_part = lax.dynamic_index_in_dim(
        goal.reshape(steps, outer, inner, per_peer, outer, inner, block), column, 2, False
    )
    goal_out = jnp.stack(
        [
            jnp.stack([goal_part[:, h, :, (h - k) % outer] for k in range(outer)], 2)
            for h in range(outer)
        ],
        0,
    )
    goal_out = jnp.transpose(goal_out, (0, 4, 1, 2, 3, 5)).reshape(
        row_count, steps, per_peer, outer * block
    )
    goal_in = lax.all_to_all(goal_out, "rows", split_axis=0, concat_axis=0, tiled=True)
    goal_in = jnp.transpose(goal_in, (1, 0, 2, 3)).reshape(steps * rows_dev, outer * block)
    gain_own = gain.reshape(outer, inner, block)[relative[hi], lo].reshape(1, outer * block)

    offsets = jnp.arange(rows_dev, dtype=jnp.int32) % K
    rows = steps * rows_dev
    place = []
    for step in range(steps):
        accepted = offsets < jnp.repeat(counts[step], K)
        slot_ids = slots[step]
        position = slot_ids // rows_dev * per_peer + slot_ids % rows_dev - source * per_peer
        place.append(
            (position[None, :] == jnp.arange(rows_dev)[:, None]) & accepted[None, :]
        )
    place = jnp.stack(place).astype(jnp.bfloat16)
    chunk = width // CHUNKS
    features = outer * block
    padded = -(-rows // LANES) * LANES
    vmem = pl.BlockSpec(memory_space=pltpu.VMEM)
    anywhere = pl.BlockSpec(memory_space=pl.ANY)
    peers = inner - 1
    dma = pltpu.SemaphoreType.DMA
    bf16 = jnp.bfloat16
    verified, trained, normed, back = pl.pallas_call(
        functools.partial(kernel, (row_count, inner, outer, steps), weight, draft),
        out_shape=(
            jax.ShapeDtypeStruct((rows, width), jnp.float32),
            jax.ShapeDtypeStruct((inner, rows, width), bf16),
            jax.ShapeDtypeStruct((rows, features), bf16),
            jax.ShapeDtypeStruct((inner, rows, features), bf16),
        ),
        in_specs=[vmem, anywhere, vmem, vmem, vmem, vmem, vmem],
        out_specs=(vmem, anywhere, vmem, vmem),
        scratch_shapes=[
            pltpu.VMEM((CHUNKS, inner, context.shape[2], chunk), bf16),
            pltpu.VMEM((CHUNKS, peers, rows, chunk), bf16),
            pltpu.VMEM((CHUNKS, peers, rows, chunk), bf16),
            pltpu.VMEM((inner, rows, width), bf16),
            pltpu.VMEM((max(outer - 1, 1), block, width), bf16),
            pltpu.VMEM((peers, rows, features), bf16),
            pltpu.VMEM((peers, rows, features), bf16),
            pltpu.VMEM((STAT_ROWS, padded), jnp.float32),
            pltpu.VMEM((peers, STAT_ROWS, padded), jnp.float32),
            pltpu.VMEM((inner, rows, features), bf16),
            dma((CHUNKS, inner)),
            dma((CHUNKS, peers)),
            dma((CHUNKS, peers)),
            dma((CHUNKS, peers)),
            dma((CHUNKS, peers)),
            dma((max(outer - 1, 1),)),
            dma((max(outer - 1, 1),)),
            dma((peers,)),
            dma((peers,)),
            dma((peers,)),
            dma((peers,)),
            dma((peers,)),
            dma((peers,)),
            dma,
        ],
        compiler_params=pltpu.CompilerParams(
            collective_id=0, has_side_effects=True, vmem_limit_bytes=56 * 1024 * 1024
        ),
    )(
        context.reshape(rows, context.shape[2]),
        o_weight,
        residual.reshape(rows, width),
        place,
        fc_weight,
        goal_in,
        gain_own,
    )
    trained = trained.reshape(inner * rows, width)
    back = back.reshape(inner * rows, features)
    grad_terms = []
    for k in range(outer):
        grad_terms.append(
            lax.dot_general(
                back[:, k * block : (k + 1) * block],
                trained,
                (((0,), (0,)), ((), ())),
                preferred_element_type=jnp.float32,
            )
        )
    grad = grad_terms[0]
    for k in range(1, outer):
        back_shift = [(b, a) for a, b in shifts[k]]
        grad = grad + lax.ppermute(
            grad_terms[k].astype(jnp.bfloat16), "rows", back_shift
        ).astype(jnp.float32)

    out = normed.reshape(steps, row_count, per_peer, outer * block)
    out = lax.all_to_all(
        jnp.transpose(out, (1, 0, 2, 3)), "rows", split_axis=0, concat_axis=0, tiled=True
    ).reshape(outer, inner, steps, per_peer, outer, block)
    out = jnp.stack(
        [
            jnp.stack([out[h, :, :, :, (h - a) % outer] for a in range(outer)], 0)
            for h in range(outer)
        ],
        0,
    )
    out = jnp.transpose(out, (1, 2, 5, 3, 0, 4))
    out = jnp.transpose(
        out.reshape(inner, draft // inner, steps, outer, per_peer), (0, 2, 3, 4, 1)
    )
    out = lax.all_to_all(out, "tensor", split_axis=0, concat_axis=0, tiled=True)
    draft_out = (
        jnp.transpose(out, (1, 2, 0, 3, 4))
        .reshape(steps, rows_dev, draft // inner)
        .astype(jnp.float32)
    )
    return (verified.reshape(steps, rows_dev, width), draft_out, grad)


def solution(mesh):
    placed = (
        P(None, "rows", "tensor"),
        P("tensor", None),
        P(None, "rows", "tensor"),
        P(None, "rows"),
        P(None, "rows"),
        P("rows", "tensor"),
        P(),
        P(None, "rows", None),
    )
    return jax.shard_map(
        local,
        mesh=mesh,
        in_specs=placed,
        out_specs=(P(None, "rows", "tensor"), P(None, "rows", "tensor"), P("rows", "tensor")),
        check_vma=False,
    )
```

```python
import functools
import math

import jax
import jax.numpy as jnp
import numpy as np
from jax import lax
from jax.experimental import pallas as pl
from jax.experimental.pallas import tpu as pltpu
from jax.sharding import PartitionSpec as P

K = 5
epsilon = 1e-06


CHUNKS = 4
LANES = 128
STAT_ROWS = 8
MESH = pl.DeviceIdType.MESH


def kernel(
    sizes, weight, draft,
    ctx, ow_hbm, res, place, fcw, goal, gain, pick,
    verified, grad, out_final,
    ow, sendp, recvp, hbuf, wbuf, sends, recvs, stat_send, stat_recv, backbuf,
    ow_sem, p_send, p_recv, h_send, h_recv, w_send, w_recv,
    s_send, s_recv, t_send, t_recv, b_send, b_recv,
    goalbuf, out_rows, out_in, out_last, gsend, grecv,
    goal_send, goal_recv, r_send, r_recv, f_send, f_recv, g_send, g_recv, own_sem, last_sem,
):
    row_count, inner, outer, steps = sizes
    rows, width = res.shape
    half = rows // steps
    chunk = width // CHUNKS
    block = fcw.shape[0]
    me = lax.axis_index("rows")
    column = lax.axis_index("tensor")
    hi = me // inner
    lo = me % inner

    def tensor_peer(j):
        return (me, (column + j) % inner)

    def lo_peer(j):
        return (hi * inner + (lo + j) % inner, column)

    def hi_peer(k):
        return ((me + k * inner) % row_count, column)

    def row_peer(d):
        return ((me + d) % row_count, column)

    order = [inner // 2] + [j for j in range(1, inner) if j != inner // 2]

    def ow_copy(c, j):
        owner = (column + j) % inner
        start = pl.multiple_of(owner * width + c * chunk, chunk)
        return pltpu.make_async_copy(
            ow_hbm.at[:, pl.ds(start, chunk)], ow.at[c, j], ow_sem.at[c, j]
        )

    for c in range(CHUNKS):
        for j in order + [0]:
            ow_copy(c, j).start()

    barrier = pltpu.get_barrier_semaphore()
    for j in range(1, inner):
        pl.semaphore_signal(barrier, inc=1, device_id=tensor_peer(j), device_id_type=MESH)
    for d in range(1, row_count):
        pl.semaphore_signal(barrier, inc=1, device_id=row_peer(d), device_id_type=MESH)
    pl.semaphore_wait(barrier, inner + row_count - 2)

    def remote(src, dst, send_sem, recv_sem, device):
        return pltpu.make_async_remote_copy(
            src_ref=src, dst_ref=dst, send_sem=send_sem, recv_sem=recv_sem,
            device_id=device, device_id_type=MESH,
        )

    def w_copy(k):
        return remote(fcw, wbuf.at[k - 1], w_send.at[k - 1], w_recv.at[k - 1], hi_peer(k))

    def p_copy(c, j):
        return remote(
            sendp.at[c, j - 1], recvp.at[c, j - 1], p_send.at[c, j - 1], p_recv.at[c, j - 1],
            tensor_peer(j),
        )

    def h_copy(c, j, owner):
        part = hbuf.at[owner, :, pl.ds(c * chunk, chunk)]
        return remote(part, part, h_send.at[c, j - 1], h_recv.at[c, j - 1], lo_peer(j))

    def s_copy(j):
        return remote(
            sends.at[j - 1], recvs.at[j - 1], s_send.at[j - 1], s_recv.at[j - 1], tensor_peer(j)
        )

    def t_copy(j):
        return remote(
            stat_send, stat_recv.at[j - 1], t_send.at[j - 1], t_recv.at[j - 1], lo_peer(j)
        )

    def b_copy(j, owner):
        return remote(
            backbuf.at[owner], backbuf.at[owner], b_send.at[j - 1], b_recv.at[j - 1],
            tensor_peer(j),
        )

    slot = goal.shape[1]
    per_owner = out_final.shape[2]

    def goal_copy(d, landing):
        return remote(
            goal.at[(me + d) % row_count], goalbuf.at[landing],
            goal_send.at[d - 1], goal_recv.at[d - 1], row_peer(d),
        )

    def r_copy(d, landing):
        return remote(
            out_rows.at[(me + d) % row_count], out_in.at[landing],
            r_send.at[d - 1], r_recv.at[d - 1], row_peer(d),
        )

    def final_source(j, h, sub):
        first = per_owner * ((column + j) % inner)
        return out_in.at[
            h * inner + first % inner + sub, (h - first // inner + outer) % outer
        ]

    def f_copy(j, h, sub, landing):
        return remote(
            final_source(j, h, sub), out_last.at[landing, h, sub],
            f_send.at[j - 1, h, sub], f_recv.at[j - 1, h, sub], tensor_peer(j),
        )

    def g_copy(k, c):
        return remote(
            gsend.at[k - 1, c], grecv.at[k - 1, c], g_send.at[k - 1, c], g_recv.at[k - 1, c],
            ((me - k * inner + row_count) % row_count, column),
        )

    own_goal = pltpu.make_async_copy(goal.at[me], goalbuf.at[me], own_sem.at[0])
    own_goal.start()
    for d in range(1, row_count):
        goal_copy(d, me).start()
    for k in range(1, outer):
        w_copy(k).start()

    def product(c, j):
        ow_copy(c, j).wait()
        return jnp.dot(ctx[...], ow[c, j], preferred_element_type=jnp.float32).astype(
            jnp.bfloat16
        )

    def finish(c):
        cols = pl.ds(c * chunk, chunk)
        total = product(c, 0).astype(jnp.float32)
        for j in range(1, inner):
            p_copy(c, j).wait_recv()
            total = total + recvp[c, j - 1].astype(jnp.float32)
        total = total + res[:, cols].astype(jnp.float32)
        verified[:, cols] = total
        hidden = total.astype(jnp.bfloat16)
        for step in range(steps):
            hbuf[lo, pl.ds(step * half, half), cols] = jnp.dot(
                place[step], hidden[step * half : (step + 1) * half],
                preferred_element_type=jnp.float32,
            ).astype(jnp.bfloat16)
        for j in range(1, inner):
            h_copy(c, j, lo).start()

    for c in range(CHUNKS):
        for j in order:
            sendp[c, j - 1] = product(c, j)
            p_copy(c, j).start()
        if c >= 1:
            finish(c - 1)
    finish(CHUNKS - 1)

    for j in range(1, inner):
        for c in range(CHUNKS):
            h_copy(c, j, (lo - j + inner) % inner).wait_recv()
    for k in range(1, outer):
        w_copy(k).wait_recv()

    def sums(j):
        mine = hbuf[(column + j) % inner]
        parts = [
            lax.dot_general(
                mine, w, (((1,), (1,)), ((), ())), preferred_element_type=jnp.float32
            )
            for w in [fcw[...]] + [wbuf[k - 1] for k in range(1, outer)]
        ]
        return jnp.concatenate(parts, 1).astype(jnp.bfloat16)

    for j in order:
        sends[j - 1] = sums(j)
        s_copy(j).start()
    summed = sums(0).astype(jnp.float32)
    for j in range(1, inner):
        s_copy(j).wait_recv()
        summed = summed + recvs[j - 1].astype(jnp.float32)
    own_goal.wait()
    for d in range(1, row_count):
        goal_copy(d, (me - d + row_count) % row_count).wait_recv()
    goal_rows = jnp.dot(
        pick[...],
        goalbuf[...].reshape(row_count * slot, goal.shape[2]),
        preferred_element_type=jnp.float32,
    )
    gains = gain[...]
    scaled = summed * gains
    lane = lax.broadcasted_iota(jnp.int32, (rows, LANES), 1)
    stats = jnp.where(
        lane == 0,
        jnp.sum(summed * summed, -1, keepdims=True),
        jnp.where(
            lane == 1,
            jnp.sum(scaled * scaled, -1, keepdims=True),
            jnp.sum(scaled * goal_rows, -1, keepdims=True),
        ),
    )
    padded = stat_send.shape[1]
    if padded > rows:
        stats = jnp.concatenate([stats, jnp.zeros((padded - rows, LANES), jnp.float32)], 0)
    stat_send[...] = jnp.transpose(stats)[:STAT_ROWS]
    for j in range(1, inner):
        t_copy(j).start()
    total = stat_send[...]
    for j in range(1, inner):
        t_copy(j).wait_recv()
        total = total + stat_recv[j - 1]
    total = jnp.transpose(
        jnp.concatenate([total, jnp.zeros((LANES - STAT_ROWS, padded), jnp.float32)], 0)
    )[:rows]
    inverse = lax.rsqrt(total[:, 0:1] / draft + epsilon)
    spread = weight * (inverse * total[:, 1:2] - total[:, 2:3]) / draft
    normed = scaled * inverse
    pulled = gains * (weight * (normed - goal_rows))
    backbuf[column] = (inverse * (pulled - summed * (inverse * inverse) * spread)).astype(
        jnp.bfloat16
    )
    for j in range(1, inner):
        b_copy(j, column).start()
    rounded = normed.astype(jnp.bfloat16)
    for k in range(outer):
        out_rows[:, k] = (
            lax.dot_general(
                pick[...], rounded[:, k * block : (k + 1) * block],
                (((0,), (0,)), ((), ())), preferred_element_type=jnp.float32,
            )
            .astype(jnp.bfloat16)
            .reshape(row_count, slot, block)
        )
    for j in range(1, inner):
        b_copy(j, (column - j + inner) % inner).wait_recv()
    back = backbuf[...].reshape(inner * rows, outer * block)

    def gradient(k, c):
        inputs = hbuf[:, :, c * chunk : (c + 1) * chunk].reshape(inner * rows, chunk)
        return lax.dot_general(
            back[:, k * block : (k + 1) * block], inputs,
            (((0,), (0,)), ((), ())), preferred_element_type=jnp.float32,
        )

    for c in range(CHUNKS):
        for k in range(1, outer):
            gsend[k - 1, c] = gradient(k, c).astype(jnp.bfloat16)
            g_copy(k, c).start()
        if c == 0:
            own_rows = pltpu.make_async_copy(out_rows.at[me], out_in.at[me], own_sem.at[1])
            own_rows.start()
            for d in range(1, row_count):
                r_copy(d, me).start()
    for c in range(CHUNKS):
        grad[:, c * chunk : (c + 1) * chunk] = gradient(0, c)
    own_rows.wait()
    for d in range(1, row_count):
        r_copy(d, (me - d + row_count) % row_count).wait_recv()
    own_last = []
    for h in range(outer):
        for sub in range(per_owner):
            own_last.append(
                pltpu.make_async_copy(
                    final_source(0, h, sub), out_last.at[column, h, sub], last_sem.at[h, sub]
                )
            )
            own_last[-1].start()
            for j in range(1, inner):
                f_copy(j, h, sub, column).start()
    for c in range(CHUNKS):
        cols = pl.ds(c * chunk, chunk)
        part = grad[:, cols]
        for k in range(1, outer):
            g_copy(k, c).wait_recv()
            part = part + grecv[k - 1, c].astype(jnp.float32)
        grad[:, cols] = part
    for copy in own_last:
        copy.wait()
    for j in range(1, inner):
        for h in range(outer):
            for sub in range(per_owner):
                f_copy(j, h, sub, (column - j + inner) % inner).wait_recv()
                f_copy(j, h, sub, column).wait_send()
    out_final[...] = out_last[...]

    for d in range(1, row_count):
        goal_copy(d, me).wait_send()
        r_copy(d, me).wait_send()
    for k in range(1, outer):
        for c in range(CHUNKS):
            g_copy(k, c).wait_send()
    for k in range(1, outer):
        w_copy(k).wait_send()
    for j in range(1, inner):
        for c in range(CHUNKS):
            p_copy(c, j).wait_send()
            h_copy(c, j, lo).wait_send()
        s_copy(j).wait_send()
        t_copy(j).wait_send()
        b_copy(j, column).wait_send()


def local(context, o_weight, residual, counts, slots, fc_weight, gain, goal):
    steps = context.shape[0]
    row_count = lax.axis_size("rows")
    inner = lax.axis_size("tensor")
    outer = row_count // inner
    rows_dev = context.shape[1]
    width = residual.shape[2]
    block = fc_weight.shape[0]
    draft = goal.shape[2]
    per_peer = rows_dev // row_count
    source = lax.axis_index("rows")
    column = lax.axis_index("tensor")
    hi = source // inner
    lo = source % inner
    weight = 1.0 / math.sqrt(steps * rows_dev * row_count)

    relative = (jnp.arange(outer)[:, None] - jnp.arange(outer)[None, :]) % outer
    goal_part = lax.dynamic_index_in_dim(
        goal.reshape(steps, outer, inner, per_peer, outer, inner, block), column, 2, False
    )
    goal_out = jnp.stack(
        [
            jnp.stack([goal_part[:, h, :, (h - k) % outer] for k in range(outer)], 2)
            for h in range(outer)
        ],
        0,
    )
    goal_out = jnp.transpose(goal_out, (0, 4, 1, 2, 3, 5))
    slot = -(-steps * per_peer // 16) * 16
    goal_out = jnp.pad(
        goal_out.reshape(row_count, steps * per_peer, outer * block),
        ((0, 0), (0, slot - steps * per_peer), (0, 0)),
    )
    index = np.arange(steps * rows_dev)
    where = index % rows_dev // per_peer * slot + index // rows_dev * per_peer + index % per_peer
    pick = jnp.asarray(where[:, None] == np.arange(row_count * slot)[None, :], jnp.bfloat16)
    gain_own = gain.reshape(outer, inner, block)[relative[hi], lo].reshape(1, outer * block)

    offsets = jnp.arange(rows_dev, dtype=jnp.int32) % K
    rows = steps * rows_dev
    place = []
    for step in range(steps):
        accepted = offsets < jnp.repeat(counts[step], K)
        slot_ids = slots[step]
        position = slot_ids // rows_dev * per_peer + slot_ids % rows_dev - source * per_peer
        place.append(
            (position[None, :] == jnp.arange(rows_dev)[:, None]) & accepted[None, :]
        )
    place = jnp.stack(place).astype(jnp.bfloat16)
    chunk = width // CHUNKS
    features = outer * block
    padded = -(-rows // LANES) * LANES
    vmem = pl.BlockSpec(memory_space=pltpu.VMEM)
    anywhere = pl.BlockSpec(memory_space=pl.ANY)
    peers = inner - 1
    dma = pltpu.SemaphoreType.DMA
    bf16 = jnp.bfloat16
    per_owner = draft // inner // block
    between = max(outer - 1, 1)
    verified, grad, out = pl.pallas_call(
        functools.partial(kernel, (row_count, inner, outer, steps), weight, draft),
        out_shape=(
            jax.ShapeDtypeStruct((rows, width), jnp.float32),
            jax.ShapeDtypeStruct((block, width), jnp.float32),
            jax.ShapeDtypeStruct((inner, outer, per_owner, slot, block), bf16),
        ),
        in_specs=[vmem, anywhere, vmem, vmem, vmem, vmem, vmem, vmem],
        out_specs=(vmem, vmem, vmem),
        scratch_shapes=[
            pltpu.VMEM((CHUNKS, inner, context.shape[2], chunk), bf16),
            pltpu.VMEM((CHUNKS, peers, rows, chunk), bf16),
            pltpu.VMEM((CHUNKS, peers, rows, chunk), bf16),
            pltpu.VMEM((inner, rows, width), bf16),
            pltpu.VMEM((max(outer - 1, 1), block, width), bf16),
            pltpu.VMEM((peers, rows, features), bf16),
            pltpu.VMEM((peers, rows, features), bf16),
            pltpu.VMEM((STAT_ROWS, padded), jnp.float32),
            pltpu.VMEM((peers, STAT_ROWS, padded), jnp.float32),
            pltpu.VMEM((inner, rows, features), bf16),
            dma((CHUNKS, inner)),
            dma((CHUNKS, peers)),
            dma((CHUNKS, peers)),
            dma((CHUNKS, peers)),
            dma((CHUNKS, peers)),
            dma((max(outer - 1, 1),)),
            dma((max(outer - 1, 1),)),
            dma((peers,)),
            dma((peers,)),
            dma((peers,)),
            dma((peers,)),
            dma((peers,)),
            dma((peers,)),
            pltpu.VMEM((row_count, slot, features), bf16),
            pltpu.VMEM((row_count, outer, slot, block), bf16),
            pltpu.VMEM((row_count, outer, slot, block), bf16),
            pltpu.VMEM((inner, outer, per_owner, slot, block), bf16),
            pltpu.VMEM((between, CHUNKS, block, chunk), bf16),
            pltpu.VMEM((between, CHUNKS, block, chunk), bf16),
            dma((row_count - 1,)),
            dma((row_count - 1,)),
            dma((row_count - 1,)),
            dma((row_count - 1,)),
            dma((peers, outer, per_owner)),
            dma((peers, outer, per_owner)),
            dma((between, CHUNKS)),
            dma((between, CHUNKS)),
            dma((2,)),
            dma((outer, per_owner)),
        ],
        compiler_params=pltpu.CompilerParams(
            collective_id=0, has_side_effects=True, vmem_limit_bytes=56 * 1024 * 1024
        ),
    )(
        context.reshape(rows, context.shape[2]),
        o_weight,
        residual.reshape(rows, width),
        place,
        fc_weight,
        goal_out,
        gain_own,
        pick,
    )
    out = out[:, :, :, : steps * per_peer].reshape(
        inner, outer, per_owner, steps, per_peer, block
    )
    draft_out = (
        jnp.transpose(out, (3, 1, 0, 4, 2, 5))
        .reshape(steps, rows_dev, draft // inner)
        .astype(jnp.float32)
    )
    return (verified.reshape(steps, rows_dev, width), draft_out, grad)


def solution(mesh):
    placed = (
        P(None, "rows", "tensor"),
        P("tensor", None),
        P(None, "rows", "tensor"),
        P(None, "rows"),
        P(None, "rows"),
        P("rows", "tensor"),
        P(),
        P(None, "rows", None),
    )
    return jax.shard_map(
        local,
        mesh=mesh,
        in_specs=placed,
        out_specs=(P(None, "rows", "tensor"), P(None, "rows", "tensor"), P("rows", "tensor")),
        check_vma=False,
    )
```
